512 devices in a mesh: pop: 32 (over x, y), mp: 16 (over z, core).
Axes of the slice: x: 4, y: 8, z: 8, core: 2. Of those that a mesh axis runs over, the one named last changes fastest.
Arguments:
- prompt_states: bfloat16 [512, 256, 3584], P(('pop', 'mp')), may hold values from -192 to 192
- norm_gain: float32 [3584], replicated, may hold values from 0.1 to 1.9
- kv_weight: bfloat16 [3584, 1024], P('mp'), may hold values from -0.09375 to 0.09375
- probe_keys: float32 [4, 128], replicated, may hold values from -6 to 6
- probe_values: float32 [4, 128], replicated, may hold values from -6 to 6
- down_factors: bfloat16 [512, 4, 3584], P(('pop', 'mp')), may hold values from -6 to 6
- up_factors: bfloat16 [512, 4, 1024], P(('pop', 'mp')), may hold values from -6 to 6
- group_ids: int32 [512], P(('pop', 'mp')), may hold values from 0 to 31, as said below
Outputs:
- fitness: float32 [512], P(('pop', 'mp'))
- update: float32 [3584, 1024], P('mp')
The draws below stay inside these ranges and needn't reach their ends.
Inputs may be any that keep to these rules, and one draw needn't show every extreme that they name: `group_ids`: each group holds exactly 16 members.
All inputs are finite; a program needn't handle non-finite values.
Results may differ from the reference program's by a relative error of at most 0.0037.
Values may be sent and summed in bfloat16 or wider, within the bound.
No kernel may reach another device: no remote copies, remote signals or barrier semaphores. Data moves between devices by JAX's collectives and lax.ppermute only.
A program may use at most 64 MiB of HBM per device.

```python
import math
import jax
import jax.numpy as jnp
from jax import lax

D = 3584
KV_HEADS = 4
HEAD = 128
KV = 1024
RANK = 4
TOK_DEV = 256
GROUP_MEMBERS = 16
MEMBERS = 512
GROUPS = 32


def draw_prompt_states(key, part):
    key = jax.random.fold_in(key, 11)
    first, second = jax.random.split(key, 2)
    shape = (MEMBERS, TOK_DEV, D)
    scales = jnp.exp(jax.random.uniform(second, (MEMBERS, TOK_DEV, 1), jnp.float32, 0.0, math.log(10.0)))
    values = jnp.clip(jax.random.normal(first, shape, jnp.float32), -6.0, 6.0) * scales
    return values.astype(jnp.bfloat16)


def draw_group_ids(key, part):
    key = jax.random.fold_in(key, 23)
    order = jax.random.permutation(key, MEMBERS)
    return (order % GROUPS).astype(jnp.int32)


def levels(rng, dims, pieces, low, largest):
    loudness, own = 1.0, jax.random.fold_in(rng, 6)
    for dim, shards_of in pieces:
        steps = jnp.exp(jax.random.uniform(jax.random.fold_in(own, dim), (shards_of,), jnp.float32, low / len(pieces), largest / len(pieces)))
        loudness = loudness * jnp.repeat(steps, dims[dim] // shards_of).reshape([-1 if axis == dim else 1 for axis in range(len(dims))])
    return loudness


def noise(rng, shape, scale, reach, pieces=(), kind=jnp.bfloat16):
    array = scale * jax.random.normal(rng, shape, jnp.float32)
    if pieces:
        array = array * levels(rng, shape, pieces, -0.22, 0.18)
    return jnp.clip(array, -reach, reach).astype(kind)


def setup_inputs(seed: int = 0) -> dict:
    seeds = jax.random.split(jax.random.key(seed), 9)
    return {
        "prompt_states": draw_prompt_states(jax.random.fold_in(seeds[8], 71), 0),
        "norm_gain": jnp.clip(1.0 + 0.18 * jax.random.normal(seeds[1], (D,), jnp.float32), 0.1, 1.9),
        "kv_weight": noise(seeds[2], (D, KV), D ** -0.5, 0.09375, ((0, 16),)),
        "probe_keys": noise(seeds[3], (KV_HEADS, HEAD), 1.0, 6.0, (), jnp.float32),
        "probe_values": noise(seeds[4], (KV_HEADS, HEAD), 1.0, 6.0, (), jnp.float32),
        "down_factors": noise(seeds[5], (MEMBERS, RANK, D), 1.0, 6.0, ((0, 512),)),
        "up_factors": noise(seeds[6], (MEMBERS, RANK, KV), 1.0, 6.0, ((0, 512),)),
        "group_ids": draw_group_ids(jax.random.fold_in(seeds[8], 71), 0),
    }


def member_reward(states, norm_gain, kv_weight, probe_keys, probe_values, down, up):
    values_in = states.astype(jnp.float32)
    scale = lax.rsqrt(lax.optimization_barrier(jnp.mean(values_in * values_in, axis=-1, keepdims=True)) + 1e-06)
    normed = (values_in * scale * norm_gain).astype(jnp.bfloat16)
    base = jnp.dot(normed, kv_weight, preferred_element_type=jnp.float32)
    low = jnp.dot(normed, down.T, preferred_element_type=jnp.float32)
    projected = base + 0.0025 * jnp.dot(low, up.astype(jnp.float32), precision=lax.Precision.HIGHEST)
    tokens = projected.shape[0]
    half = KV_HEADS * HEAD
    keys = projected[:, :half].reshape(tokens, KV_HEADS, HEAD)
    values = projected[:, half:].reshape(tokens, KV_HEADS, HEAD)
    key_score = jnp.einsum('thd,hd->th', keys, probe_keys, precision=lax.Precision.HIGHEST) / math.sqrt(HEAD)
    value_score = jnp.einsum('thd,hd->th', values, probe_values, precision=lax.Precision.HIGHEST) / math.sqrt(HEAD)
    return jnp.sum(jnp.tanh(key_score) * value_score) / tokens

def reference(prompt_states, norm_gain, kv_weight, probe_keys, probe_values, down_factors, up_factors, group_ids):

    def one_member(items):
        return member_reward(items[0], norm_gain, kv_weight, probe_keys, probe_values, items[1], items[2])
    rewards = lax.map(one_member, (prompt_states, down_factors, up_factors))
    onehot = (group_ids[:, None] == jnp.arange(GROUPS, dtype=jnp.int32)[None, :]).astype(jnp.float32)
    sums = lax.optimization_barrier(jnp.sum(onehot * rewards[:, None], axis=0))
    baseline = sums / GROUP_MEMBERS
    centered = rewards - lax.optimization_barrier(jnp.sum(onehot * baseline[None, :], axis=1))
    spread = jnp.sum(centered * centered) / MEMBERS
    fitness = centered / jnp.sqrt(spread + 1e-05)
    weighted = (fitness[:, None, None] * down_factors.astype(jnp.float32)).reshape(MEMBERS * RANK, D)
    columns = up_factors.astype(jnp.float32).reshape(MEMBERS * RANK, KV)
    update = lax.dot_general(weighted, columns, (((0,), (0,)), ((), ())), precision=lax.Precision.HIGHEST)
    return (fitness, update / math.sqrt(RANK * MEMBERS))
```

```python
import math

import jax
import jax.numpy as jnp
from jax import lax
from jax.experimental import pallas as pl
from jax.experimental.pallas import tpu as pltpu
from jax.sharding import Mesh
from jax.sharding import PartitionSpec as P

KV_HEADS = 4
HEAD = 128
RANK = 4
GROUP_MEMBERS = 16
LANES = 128
SUBLANES = 8
XY = ("x", "y")
ZC = ("z", "core")
ALL = ("x", "y", "z", "core")
VMEM = pl.BlockSpec(memory_space=pltpu.VMEM)
SMEM = pl.BlockSpec(memory_space=pltpu.SMEM)
F32 = jnp.float32
BF16 = jnp.bfloat16
CONTRACT_LANES = (((1,), (1,)), ((), ()))
CONTRACT_ROWS = (((0,), (0,)), ((), ()))


def three_parts(value):
    high = value.astype(BF16)
    rest = value - high.astype(F32)
    middle = rest.astype(BF16)
    low = rest - middle.astype(F32)
    return jnp.concatenate([high.astype(F32), middle.astype(F32), low], axis=0).astype(BF16)


def sum_parts(product):
    rows = product.shape[0] // 3
    return product[:rows] + (product[rows : 2 * rows] + product[2 * rows :])


def iota(shape, axis):
    return lax.broadcasted_iota(jnp.int32, shape, axis)


def one_hot(condition):
    return jnp.where(condition, 1.0, 0.0).astype(BF16)


def probe_kernel(weight, probe_keys, probe_values, up, down, weight_probe, up_probe, factors):
    copies, _, rows = weight_probe.shape
    probes = jnp.concatenate([probe_keys[...], probe_values[...]], axis=0)
    heads = probes.shape[0]
    wide = jnp.concatenate([probes] * heads, axis=1)
    own = iota(wide.shape, 1) // HEAD == iota(wide.shape, 0)
    probes = three_parts(jnp.where(own, wide, 0.0))
    product = sum_parts(lax.dot_general(probes, weight[...], CONTRACT_LANES, preferred_element_type=F32))
    weight_probe[...] = jnp.broadcast_to(product[None], weight_probe.shape)
    up_probe[...] = sum_parts(lax.dot_general(probes, up[...], CONTRACT_LANES, preferred_element_type=F32))

    half = up.shape[1] // 2
    select = iota((2 * RANK, RANK), 0), iota((2 * RANK, RANK), 1)
    upper = one_hot(select[0] == select[1])
    lower = one_hot(select[0] == select[1] + RANK)

    def place(which, block):
        return jnp.dot(which, block, preferred_element_type=F32)

    ups = (place(upper, up[:, :half]) + place(lower, up[:, half:])).astype(BF16)
    first = place(upper, down[...])
    second = place(lower, down[...])
    spare = jnp.zeros((2 * RANK, LANES), F32)
    second = jnp.concatenate([second, spare], axis=1)
    for i in range(copies):
        start = i * rows
        downs = first[:, start : start + LANES] + second[:, start + LANES : start + 2 * LANES]
        factors[i, :, :half] = ups
        factors[i, :, half:] = downs.astype(BF16)


def norm_kernel(states, gain, down, normed, low):
    values = states[...].astype(F32)
    scale = lax.rsqrt(jnp.mean(values * values, axis=-1, keepdims=True) + 1e-06)
    normed[...] = (values * scale * gain[...]).astype(BF16)
    low[...] = lax.dot_general(down[...], normed[...], CONTRACT_LANES, preferred_element_type=F32)


def reward_kernel(place, normed, low, weight_probe, up_probe, out):
    members = out.shape[0]
    probe = jnp.concatenate([weight_probe[i] for i in range(members)], axis=1)
    score = sum_parts(lax.dot_general(three_parts(probe), normed[...], CONTRACT_LANES, preferred_element_type=F32))
    extra = up_probe[:, 0:1] * low[0:1, :]
    for i in range(1, RANK):
        extra = extra + up_probe[:, i : i + 1] * low[i : i + 1, :]
    score = (score + 0.0025 * extra) * (1.0 / math.sqrt(HEAD))
    terms = jnp.tanh(score[:KV_HEADS]) * score[KV_HEADS:]
    reward = jnp.sum(jnp.sum(terms, axis=1, keepdims=True), axis=0, keepdims=True) * (1.0 / terms.shape[1])
    lane = iota(out.shape[1:], 1)
    group = place[2].astype(F32)
    row = jnp.where(lane == place[1], reward, 0.0) + jnp.where(lane == place[1] + members, group, 0.0)
    out[...] = jnp.broadcast_to(row[None], out.shape)


def relay_kernel(place, rows, out):
    row = jnp.sum(rows[...], axis=0)
    mine = iota(row.shape, 0) == place[0] % SUBLANES
    out[...] = jnp.broadcast_to(jnp.where(mine, row, 0.0)[None], out.shape)


def pack_kernel(factors, pieces):
    members, packed, width = factors.shape
    rows = members * packed
    count = members * RANK
    flat = factors[...].astype(F32).reshape(rows, width).astype(BF16)
    target = iota((rows, rows), 0)
    source = iota((rows, rows), 1)
    wanted = target % count // RANK * packed + target // count * RANK + target % RANK
    flat = jnp.dot(one_hot(source == wanted), flat, preferred_element_type=F32)
    half = width - LANES
    down = jnp.concatenate([flat[:count, half:], flat[count:, half:]], axis=1)
    targets = pieces.shape[0]
    column_parts = 2 * half // LANES
    row_parts = targets // column_parts
    share = (pieces.shape[2] - 16) // 2
    spare = jnp.zeros((count // 2, SUBLANES), F32)
    for i in range(row_parts):
        mine = down[:, i * share : (i + 1) * share]
        mine = jnp.concatenate([mine[: count // 2], spare, mine[count // 2 :], spare], axis=1).astype(BF16)
        for j in range(column_parts):
            first_row = j // (column_parts // 2) * count
            column = j % (column_parts // 2) * LANES
            columns = flat[first_row : first_row + count, column : column + LANES]
            pieces[i * column_parts + j, :count, :] = columns.astype(BF16)
            pieces[i * column_parts + j, count:, :] = mine


def update_kernel(place, rows, pieces, fitness, out):
    sources = rows.shape[0]
    table = jnp.sum(rows[...].reshape(sources // SUBLANES, SUBLANES, SUBLANES, LANES), axis=1)
    table = table.reshape(sources, LANES)
    count = pieces.shape[1] * 2 // 3
    members = count // RANK
    lane = iota(table.shape, 1)
    reward = jnp.where(lane < members, table, 0.0)
    group = jnp.where(lane < members, pltpu.roll(table, LANES - members, axis=1), -1.0)
    total = sources * members
    sums = [
        jnp.sum(jnp.where(group == float(i), reward, 0.0), axis=0, keepdims=True)
        for i in range(total // GROUP_MEMBERS)
    ]
    sums = jnp.sum(jnp.concatenate(sums, axis=0), axis=1, keepdims=True) * (1.0 / GROUP_MEMBERS)
    baseline = jnp.zeros_like(reward)
    for i in range(total // GROUP_MEMBERS):
        baseline = jnp.where(group == float(i), sums[i : i + 1, :], baseline)
    centered = jnp.where(lane < members, reward - baseline, 0.0)
    spread = jnp.sum(jnp.sum(centered * centered, axis=1, keepdims=True), axis=0, keepdims=True) * (1.0 / total)
    shaped = centered / jnp.sqrt(spread + 1e-05)
    own = jnp.where((iota(table.shape, 0) == place[0]) & (lane == place[1]), shaped, 0.0)
    fitness[...] = jnp.sum(jnp.sum(own, axis=1, keepdims=True), axis=0, keepdims=True)

    chosen = iota((count, LANES), 1) == iota((count, LANES), 0) // RANK
    weights = jnp.where(chosen[None], jnp.broadcast_to(shaped[:, None, :], (sources, count, LANES)), 0.0)
    weights = jnp.sum(weights, axis=2, keepdims=True)
    weighted = pieces[:, :count, :].astype(F32) * weights
    high = weighted.astype(BF16)
    low = (weighted - high.astype(F32)).astype(BF16)
    part = count // 2
    flat = sources * part
    columns = [
        block[:, start : start + part, :].reshape(flat, LANES) for start in (0, part) for block in (high, low)
    ]
    downs = pieces[:, count:, :].reshape(flat, LANES)
    product = lax.dot_general(downs, jnp.concatenate(columns, axis=1), CONTRACT_ROWS, preferred_element_type=F32)
    middle = LANES // 2
    first = product[:middle, :LANES] + product[:middle, LANES : 2 * LANES]
    second = product[middle:, 2 * LANES : 3 * LANES] + product[middle:, 3 * LANES :]
    block = ((first + second) * (1.0 / math.sqrt(RANK * total))).astype(BF16)
    out[...] = jnp.broadcast_to(block[None], out.shape)


def assemble_kernel(blocks, out):
    sources = blocks.shape[0]
    column_parts = out.shape[1] // LANES
    share = out.shape[0] * column_parts // sources
    for i in range(sources):
        row, column = i // column_parts * share, i % column_parts * LANES
        out[row : row + share, column : column + LANES] = blocks[i].astype(F32)[:share]


def call(kernel, out_shape, in_specs, *operands):
    many = isinstance(out_shape, (list, tuple))
    return pl.pallas_call(
        kernel,
        out_shape=out_shape,
        in_specs=in_specs,
        out_specs=[VMEM] * len(out_shape) if many else VMEM,
        compiler_params=pltpu.CompilerParams(vmem_limit_bytes=40 * 1024 * 1024),
    )(*operands)


def exchange(array, axes):
    return lax.all_to_all(array, axes, split_axis=0, concat_axis=0, tiled=True)


def local(
    prompt_states,
    norm_gain,
    kv_weight,
    probe_keys,
    probe_values,
    down_factors,
    up_factors,
    group_ids,
):
    pop = lax.axis_size(XY)
    mp = lax.axis_size(ZC)
    place = jnp.stack([lax.axis_index(XY), lax.axis_index(ZC), group_ids[0]]).astype(jnp.int32)
    states, down, up = prompt_states[0], down_factors[0], up_factors[0]
    tokens, width = states.shape
    columns = up.shape[1]
    rows = width // mp
    heads = 2 * KV_HEADS
    weight_probe, up_probe, factors = call(
        probe_kernel,
        [
            jax.ShapeDtypeStruct((mp, heads, rows), F32),
            jax.ShapeDtypeStruct((heads, RANK), F32),
            jax.ShapeDtypeStruct((mp, 2 * RANK, columns // 2 + LANES), BF16),
        ],
        [VMEM] * 5,
        kv_weight,
        probe_keys,
        probe_values,
        up,
        down,
    )
    weight_probe = exchange(weight_probe, ZC)
    factors = exchange(factors, ZC)
    normed, low = call(
        norm_kernel,
        [jax.ShapeDtypeStruct((tokens, width), BF16), jax.ShapeDtypeStruct((RANK, tokens), F32)],
        [VMEM] * 3,
        states,
        norm_gain[None],
        down,
    )
    reward = call(
        reward_kernel,
        jax.ShapeDtypeStruct((mp, SUBLANES, LANES), F32),
        [SMEM] + [VMEM] * 4,
        place,
        normed,
        low,
        weight_probe,
        up_probe,
    )
    reward = exchange(reward, ZC)
    count = mp * RANK
    pieces = call(pack_kernel, jax.ShapeDtypeStruct((pop, count * 3 // 2, LANES), BF16), [VMEM], factors)
    pieces = exchange(pieces, XY)
    reward = call(
        relay_kernel, jax.ShapeDtypeStruct((pop, SUBLANES, LANES), F32), [SMEM, VMEM], place, reward
    )
    reward = exchange(reward, XY)
    fitness, blocks = call(
        update_kernel,
        [jax.ShapeDtypeStruct((1, 1), F32), jax.ShapeDtypeStruct((pop, LANES // 2, LANES), BF16)],
        [SMEM, VMEM, VMEM],
        place,
        reward,
        pieces,
    )
    blocks = exchange(blocks, XY)
    update = call(assemble_kernel, jax.ShapeDtypeStruct((rows, columns), F32), [VMEM], blocks)
    return (fitness.reshape(1), update)


def solution(mesh):
    grid = Mesh(mesh.devices.reshape(4, 8, 8, 2), ALL)
    in_specs = (
        P(ALL, None, None),
        P(),
        P(ZC, None),
        P(),
        P(),
        P(ALL, None, None),
        P(ALL, None, None),
        P(ALL),
    )
    out_specs = (P(ALL), P(ZC, None))
    return jax.shard_map(local, mesh=grid, in_specs=in_specs, out_specs=out_specs, check_vma=False)
```

```python
import math

import jax
import jax.numpy as jnp
from jax import lax
from jax.experimental import pallas as pl
from jax.experimental.pallas import tpu as pltpu
from jax.sharding import Mesh
from jax.sharding import PartitionSpec as P

KV_HEADS = 4
HEAD = 128
RANK = 4
GROUP_MEMBERS = 16
LANES = 128
SUBLANES = 8
XY = ("x", "y")
ZC = ("z", "core")
ALL = ("x", "y", "z", "core")
VMEM = pl.BlockSpec(memory_space=pltpu.VMEM)
SMEM = pl.BlockSpec(memory_space=pltpu.SMEM)
F32 = jnp.float32
BF16 = jnp.bfloat16
CONTRACT_LANES = (((1,), (1,)), ((), ()))
CONTRACT_ROWS = (((0,), (0,)), ((), ()))


def bf16_parts(value, count):
    parts = []
    for _ in range(count):
        part = value.astype(BF16).astype(F32)
        parts.append(part)
        value = value - part
    return parts


def iota(shape, axis):
    return lax.broadcasted_iota(jnp.int32, shape, axis)


def sum_all(value):
    return jnp.sum(jnp.sum(value, axis=1, keepdims=True), axis=0, keepdims=True)


def pair_upper(even, odd):
    return jnp.where(iota(even.shape, even.ndim - 2) < RANK, even, pltpu.roll(odd, RANK, axis=odd.ndim - 2))


def pair_lower(even, odd):
    return jnp.where(iota(even.shape, even.ndim - 2) < RANK, pltpu.roll(even, RANK, axis=even.ndim - 2), odd)


def probe_kernel(weight_hbm, keys_hbm, values_hbm, up_hbm, down_hbm, up_probe, out, *scratch):
    buffers, sems = scratch[:5], scratch[5]
    sources = (weight_hbm, keys_hbm, values_hbm, up_hbm, down_hbm)
    copies = [pltpu.make_async_copy(a, b, sems.at[i]) for i, (a, b) in enumerate(zip(sources, buffers))]
    for copy in copies:
        copy.start()
    for copy in copies:
        copy.wait()
    weight, probe_keys, probe_values, up, down = buffers
    devices, _, rows = out.shape
    probes = jnp.concatenate([probe_keys[...], probe_values[...]], axis=0)
    heads = probes.shape[0]
    wide = jnp.concatenate([probes] * heads, axis=1)
    own = iota(wide.shape, 1) // HEAD == iota(wide.shape, 0)
    probes = jnp.concatenate(bf16_parts(jnp.where(own, wide, 0.0), 3), axis=0).astype(BF16)

    def against(block):
        product = lax.dot_general(probes, block, CONTRACT_LANES, preferred_element_type=F32)
        return product[:heads] + (product[heads : 2 * heads] + product[2 * heads :])

    up_probe[...] = against(up[...])
    high, low = bf16_parts(against(weight[...]), 2)
    select = iota((SUBLANES, RANK), 0) == iota((SUBLANES, RANK), 1)
    downs = jnp.dot(jnp.where(select, 1.0, 0.0).astype(BF16), down[...], preferred_element_type=F32)
    for i in range(devices):
        block = jnp.concatenate([high, low, downs[:, i * rows : (i + 1) * rows]], axis=0)
        out[i] = block.astype(BF16)


def norm_kernel(states, gain, down, normed, low):
    values = states[...].astype(F32)
    scale = lax.rsqrt(jnp.mean(values * values, axis=-1, keepdims=True) + 1e-06)
    normed[...] = (values * scale * gain[...]).astype(BF16)
    low[...] = lax.dot_general(down[...], normed[...], CONTRACT_LANES, preferred_element_type=F32)


def reward_kernel(place, normed, low, received, up_probe, up, out):
    received = received[...].astype(F32)
    members = received.shape[0]
    heads = 2 * KV_HEADS
    probe = jnp.concatenate([received[i, : 2 * heads] for i in range(members)], axis=1).astype(BF16)
    score = lax.dot_general(probe, normed[...], CONTRACT_LANES, preferred_element_type=F32)
    score = score[:heads] + score[heads:]
    extra = up_probe[:, 0:1] * low[0:1, :]
    for i in range(1, RANK):
        extra = extra + up_probe[:, i : i + 1] * low[i : i + 1, :]
    score = (score + 0.0025 * extra) * (1.0 / math.sqrt(HEAD))
    terms = jnp.tanh(score[:KV_HEADS]) * score[KV_HEADS:]
    reward = sum_all(terms) * (1.0 / terms.shape[1])

    targets = out.shape[0]
    tile = (SUBLANES, LANES)
    lane = iota(tile, 1)
    row = jnp.where(lane == place[0] + 3 * targets, place[2].astype(F32), 0.0)
    for i, part in enumerate(bf16_parts(reward, 3)):
        row = row + jnp.where(lane == place[0] + i * targets, part, 0.0)
    row = jnp.where(iota(tile, 0) == RANK, row, 0.0)

    down = received[:, 2 * heads :]
    down = down.reshape(members // 2, 2, SUBLANES, down.shape[2])
    down = pair_upper(down[:, 0], down[:, 1]).reshape(members * RANK, down.shape[3])
    half = members * RANK // 2
    column_parts = up.shape[1] // LANES
    row_parts = targets // column_parts
    share = down.shape[1] // row_parts
    spare = jnp.zeros((half, LANES // 2 - share), F32)
    select = iota((SUBLANES, RANK), 0) == iota((SUBLANES, RANK), 1)
    ups = jnp.dot(jnp.where(select, 1.0, 0.0).astype(BF16), up[...], preferred_element_type=F32)
    for i in range(row_parts):
        mine = down[:, i * share : (i + 1) * share]
        mine = jnp.concatenate([mine[:half], spare, mine[half:], spare], axis=1)
        for j in range(column_parts):
            last = ups[:, j * LANES : (j + 1) * LANES] + row
            out[i * column_parts + j] = jnp.concatenate([mine, last], axis=0).astype(BF16)


def relay_kernel(received, out):
    last = received[...].astype(F32)
    last = last[:, last.shape[1] - SUBLANES :]
    row = jnp.sum(last, axis=0)
    last = last.reshape(last.shape[0] // 2, 2, SUBLANES, LANES)
    ups = pair_upper(last[:, 0], last[:, 1])
    block = jnp.concatenate([ups.reshape(-1, LANES), row], axis=0).astype(BF16)
    out[...] = jnp.broadcast_to(block[None], out.shape)


def order_kernel(received, out):
    sources, rows, _ = received.shape
    tiles = rows // SUBLANES - 1
    down = received[...].astype(F32)[:, : tiles * SUBLANES]
    down = down.reshape(sources // 2, 2, tiles, SUBLANES, LANES)
    upper = pair_upper(down[:, 0], down[:, 1])
    lower = pair_lower(down[:, 0], down[:, 1])
    for i in range(tiles):
        out[2 * i] = upper[:, i].reshape(-1, LANES).astype(BF16)
        out[2 * i + 1] = lower[:, i].reshape(-1, LANES).astype(BF16)


def update_kernel(place, received, down, fitness, out):
    members, rows, _ = received.shape
    received = received[...].astype(F32)
    count = rows - SUBLANES
    sources = count // RANK
    total = members * sources
    tile = iota((members, SUBLANES, LANES), 1) == RANK
    table = jnp.sum(jnp.where(tile, received[:, count:], 0.0), axis=1)
    lane = iota(table.shape, 1)
    valid = lane < sources
    second = pltpu.roll(table, LANES - sources, axis=1)
    third = pltpu.roll(table, LANES - 2 * sources, axis=1)
    reward = jnp.where(valid, table + (second + third), 0.0)
    group = jnp.where(valid, pltpu.roll(table, LANES - 3 * sources, axis=1), -1.0)
    sums = [
        jnp.sum(jnp.where(group == float(i), reward, 0.0), axis=0, keepdims=True)
        for i in range(total // GROUP_MEMBERS)
    ]
    sums = jnp.sum(jnp.concatenate(sums, axis=0), axis=1, keepdims=True) * (1.0 / GROUP_MEMBERS)
    baseline = jnp.zeros_like(reward)
    for i in range(total // GROUP_MEMBERS):
        baseline = jnp.where(group == float(i), sums[i : i + 1, :], baseline)
    centered = jnp.where(valid, reward - baseline, 0.0)
    spread = sum_all(centered * centered) * (1.0 / total)
    shaped = centered / jnp.sqrt(spread + 1e-05)
    own = jnp.where((iota(table.shape, 0) == place[1]) & (lane == place[0]), shaped, 0.0)
    fitness[...] = sum_all(own)

    chosen = iota((count, LANES), 1) == iota((count, LANES), 0) // RANK
    weights = jnp.where(chosen[None], jnp.broadcast_to(shaped[:, None, :], (members, count, LANES)), 0.0)
    weighted = received[:, :count] * jnp.sum(weights, axis=2, keepdims=True)
    high = weighted.astype(BF16)
    low = (weighted - high.astype(F32)).astype(BF16)
    half = members // 2
    flat = half * count
    columns = [block[start : start + half].reshape(flat, LANES) for start in (0, half) for block in (high, low)]
    columns = jnp.concatenate(columns, axis=1)
    downs = down[...].reshape(flat, LANES)
    product = lax.dot_general(downs, columns, CONTRACT_ROWS, preferred_element_type=F32)
    middle = LANES // 2
    first = product[:middle, :LANES] + product[:middle, LANES : 2 * LANES]
    second = product[middle:, 2 * LANES : 3 * LANES] + product[middle:, 3 * LANES :]
    block = ((first + second) * (1.0 / math.sqrt(RANK * total)))[: out.shape[1]]
    out[...] = jnp.broadcast_to(block.astype(BF16)[None], out.shape)


def assemble_kernel(blocks, out):
    sources, share, _ = blocks.shape
    column_parts = out.shape[1] // LANES
    for i in range(sources):
        row, column = i // column_parts * share, i % column_parts * LANES
        out[row : row + share, column : column + LANES] = blocks[i].astype(F32)


def call(kernel, out_shape, in_specs, *operands, scratch=(), vmem=40):
    many = isinstance(out_shape, (list, tuple))
    return pl.pallas_call(
        kernel,
        out_shape=out_shape,
        in_specs=in_specs,
        out_specs=[VMEM] * len(out_shape) if many else VMEM,
        scratch_shapes=scratch,
        compiler_params=pltpu.CompilerParams(vmem_limit_bytes=vmem * 1024 * 1024),
    )(*operands)


def exchange(array, axes):
    return lax.all_to_all(array, axes, split_axis=0, concat_axis=0, tiled=True)


def local(
    prompt_states,
    norm_gain,
    kv_weight,
    probe_keys,
    probe_values,
    down_factors,
    up_factors,
    group_ids,
):
    pop = lax.axis_size(XY)
    mp = lax.axis_size(ZC)
    place = jnp.stack([lax.axis_index(XY), lax.axis_index(ZC), group_ids[0]]).astype(jnp.int32)
    states, down, up = prompt_states[0], down_factors[0], up_factors[0]
    tokens, width = states.shape
    columns = up.shape[1]
    rows = width // mp
    share = rows * columns // (pop * LANES)
    heads = 2 * KV_HEADS
    operands = (kv_weight, probe_keys, probe_values, up, down)
    up_probe, parts = call(
        probe_kernel,
        [
            jax.ShapeDtypeStruct((heads, RANK), F32),
            jax.ShapeDtypeStruct((mp, 3 * heads, rows), BF16),
        ],
        [pl.BlockSpec(memory_space=pltpu.HBM)] * len(operands),
        *operands,
        scratch=[pltpu.VMEM(a.shape, a.dtype) for a in operands] + [pltpu.SemaphoreType.DMA((len(operands),))],
        vmem=60,
    )
    parts = exchange(parts, ZC)
    normed, low = call(
        norm_kernel,
        [jax.ShapeDtypeStruct((tokens, width), BF16), jax.ShapeDtypeStruct((RANK, tokens), F32)],
        [VMEM] * 3,
        states,
        norm_gain[None],
        down,
    )
    half = mp * RANK // 2
    pieces = call(
        reward_kernel,
        jax.ShapeDtypeStruct((pop, half + SUBLANES, LANES), BF16),
        [SMEM] + [VMEM] * 5,
        place,
        normed,
        low,
        parts,
        up_probe,
        up,
    )
    pieces = exchange(pieces, XY)
    ups = call(relay_kernel, jax.ShapeDtypeStruct((mp, pop * RANK + SUBLANES, LANES), BF16), [VMEM], pieces)
    ups = exchange(ups, ZC)
    downs = call(order_kernel, jax.ShapeDtypeStruct((mp // 2, pop * RANK, LANES), BF16), [VMEM], pieces)
    fitness, blocks = call(
        update_kernel,
        [jax.ShapeDtypeStruct((1, 1), F32), jax.ShapeDtypeStruct((pop, share, LANES), BF16)],
        [SMEM, VMEM, VMEM],
        place,
        ups,
        downs,
    )
    blocks = exchange(blocks, XY)
    update = call(assemble_kernel, jax.ShapeDtypeStruct((rows, columns), F32), [VMEM], blocks)
    return (fitness.reshape(1), update)


def solution(mesh):
    grid = Mesh(mesh.devices.reshape(4, 8, 8, 2), ALL)
    in_specs = (
        P(ALL, None, None),
        P(),
        P(ZC, None),
        P(),
        P(),
        P(ALL, None, None),
        P(ALL, None, None),
        P(ALL),
    )
    out_specs = (P(ALL), P(ZC, None))
    return jax.shard_map(local, mesh=grid, in_specs=in_specs, out_specs=out_specs, check_vma=False)
```

```python
import math

import jax
import jax.numpy as jnp
from jax import lax
from jax.experimental import pallas as pl
from jax.experimental.pallas import tpu as pltpu
from jax.sharding import Mesh
from jax.sharding import PartitionSpec as P

KV_HEADS = 4
HEAD = 128
RANK = 4
GROUP_MEMBERS = 16
LANES = 128
SUBLANES = 8
XY = ("x", "y")
ZC = ("z", "core")
ALL = ("x", "y", "z", "core")
VMEM = pl.BlockSpec(memory_space=pltpu.VMEM)
SMEM = pl.BlockSpec(memory_space=pltpu.SMEM)
F32 = jnp.float32
BF16 = jnp.bfloat16
CONTRACT_LANES = (((1,), (1,)), ((), ()))


def bf16_parts(value, count):
    parts = []
    for _ in range(count):
        part = value.astype(BF16).astype(F32)
        parts.append(part)
        value = value - part
    return parts


def iota(shape, axis):
    return lax.broadcasted_iota(jnp.int32, shape, axis)


def sum_all(value):
    return jnp.sum(jnp.sum(value, axis=1, keepdims=True), axis=0, keepdims=True)


def pair_upper(even, odd):
    return jnp.where(iota(even.shape, even.ndim - 2) < RANK, even, pltpu.roll(odd, RANK, axis=odd.ndim - 2))


def pair_lower(even, odd):
    return jnp.where(iota(even.shape, even.ndim - 2) < RANK, pltpu.roll(even, RANK, axis=even.ndim - 2), odd)


def probe_rows(probe_keys, probe_values):
    probes = jnp.concatenate([probe_keys[...], probe_values[...]], axis=0)
    wide = jnp.concatenate([probes] * probes.shape[0], axis=1)
    own = iota(wide.shape, 1) // HEAD == iota(wide.shape, 0)
    return jnp.concatenate(bf16_parts(jnp.where(own, wide, 0.0), 3), axis=0).astype(BF16)


def against_probes(block, probes):
    product = lax.dot_general(probes, block, CONTRACT_LANES, preferred_element_type=F32)
    heads = product.shape[0] // 3
    return product[:heads] + (product[heads : 2 * heads] + product[2 * heads :])


def placed(block, offset):
    shape = (SUBLANES, RANK)
    select = jnp.where(iota(shape, 0) == iota(shape, 1) + offset, 1.0, 0.0).astype(BF16)
    return jnp.dot(select, block, preferred_element_type=F32)


def probe_kernel(weight_hbm, keys_hbm, values_hbm, up_hbm, down_hbm, up_probe, out, *scratch):
    buffers, sems = scratch[:5], scratch[5]
    sources = (weight_hbm, keys_hbm, values_hbm, up_hbm, down_hbm)
    copies = [pltpu.make_async_copy(a, b, sems.at[i]) for i, (a, b) in enumerate(zip(sources, buffers))]
    for copy in copies:
        copy.start()
    weight, probe_keys, probe_values, up, down = buffers
    for copy in copies[1:]:
        copy.wait()
    probes = probe_rows(probe_keys, probe_values)
    up_probe[...] = against_probes(up[...], probes)
    devices = out.shape[0]
    rows = weight.shape[0]
    first = placed(down[...], 0)
    second = jnp.concatenate([placed(down[...], RANK), jnp.zeros((SUBLANES, LANES), F32)], axis=1)
    copies[0].wait()
    product = jnp.concatenate(bf16_parts(against_probes(weight[...], probes), 2), axis=0)
    spare = jnp.zeros((product.shape[0], 2 * LANES - rows), F32)
    product = jnp.concatenate([product[:, :LANES], jnp.concatenate([product[:, LANES:], spare], axis=1)], axis=0)
    for i in range(devices):
        start = i * rows
        block = first[:, start : start + LANES] + second[:, start + LANES : start + 2 * LANES]
        out[i] = jnp.concatenate([product, block], axis=0).astype(BF16)


def norm_kernel(states, gain, down, normed, low):
    values = states[...].astype(F32)
    scale = lax.rsqrt(jnp.mean(values * values, axis=-1, keepdims=True) + 1e-06)
    normed[...] = (values * scale * gain[...]).astype(BF16)
    low[...] = lax.dot_general(down[...], normed[...], CONTRACT_LANES, preferred_element_type=F32)


def reward_kernel(place, normed, low, received, up_probe, up, out):
    received = received[...].astype(F32)
    members = received.shape[0]
    heads = 2 * KV_HEADS
    rest = normed.shape[1] // members - LANES
    probe = []
    for i in range(members):
        probe += [received[i, : 2 * heads], received[i, 2 * heads : 4 * heads, :rest]]
    probe = jnp.concatenate(probe, axis=1).astype(BF16)
    score = lax.dot_general(probe, normed[...], CONTRACT_LANES, preferred_element_type=F32)
    score = score[:heads] + score[heads:]
    extra = up_probe[:, 0:1] * low[0:1, :]
    for i in range(1, RANK):
        extra = extra + up_probe[:, i : i + 1] * low[i : i + 1, :]
    score = (score + 0.0025 * extra) * (1.0 / math.sqrt(HEAD))
    terms = jnp.tanh(score[:KV_HEADS]) * score[KV_HEADS:]
    reward = sum_all(terms) * (1.0 / terms.shape[1])

    targets = out.shape[0]
    tile = (SUBLANES, LANES)
    lane = iota(tile, 1)
    row = jnp.where(lane == place[0] + 3 * targets, place[2].astype(F32), 0.0)
    for i, part in enumerate(bf16_parts(reward, 3)):
        row = row + jnp.where(lane == place[0] + i * targets, part, 0.0)
    row = jnp.where(iota(tile, 0) == RANK, row, 0.0)

    down = received[:, 4 * heads :].reshape(members // 2, 2, SUBLANES, LANES)
    first = pair_upper(down[:, 0], down[:, 1]).reshape(members * RANK, LANES)
    second = pair_lower(down[:, 0], down[:, 1]).reshape(members * RANK, LANES)
    down = jnp.concatenate([first, second[:, :rest]], axis=1)
    half = members * RANK // 2
    column_parts = up.shape[1] // LANES
    row_parts = targets // column_parts
    share = down.shape[1] // row_parts
    spare = jnp.zeros((half, LANES // 2 - share), F32)
    ups = placed(up[...], 0)
    for i in range(row_parts):
        mine = down[:, i * share : (i + 1) * share]
        mine = jnp.concatenate([mine[:half], spare, mine[half:], spare], axis=1)
        for j in range(column_parts):
            last = ups[:, j * LANES : (j + 1) * LANES] + row
            out[i * column_parts + j] = jnp.concatenate([mine, last], axis=0).astype(BF16)


def relay_kernel(received, out):
    last = received[...].astype(F32)
    last = last[:, last.shape[1] - SUBLANES :]
    row = jnp.sum(last, axis=0)
    last = last.reshape(last.shape[0] // 2, 2, SUBLANES, LANES)
    ups = pair_upper(last[:, 0], last[:, 1])
    block = jnp.concatenate([ups.reshape(-1, LANES), row], axis=0).astype(BF16)
    out[...] = jnp.broadcast_to(block[None], out.shape)


def order_kernel(received, out):
    sources, rows, _ = received.shape
    tiles = rows // SUBLANES - 1
    down = received[...].astype(F32)[:, : tiles * SUBLANES]
    down = down.reshape(sources // 2, 2, tiles, SUBLANES, LANES)
    upper = pair_upper(down[:, 0], down[:, 1])
    lower = pair_lower(down[:, 0], down[:, 1])
    ordered = [half[:, i].reshape(-1, LANES) for i in range(tiles) for half in (upper, lower)]
    out[...] = jnp.transpose(jnp.concatenate(ordered, axis=0)).astype(BF16)


def update_kernel(place, own, other, down, fitness, out):
    chips, rows, _ = own.shape
    members = 2 * chips
    own, other = own[...].astype(F32), other[...].astype(F32)
    first_core = place[1] % 2 == 0
    cores = [jnp.where(first_core, own, other), jnp.where(first_core, other, own)]
    received = jnp.stack(cores, axis=1).reshape(members, rows, LANES)
    count = rows - SUBLANES
    sources = count // RANK
    total = members * sources
    tile = iota((members, SUBLANES, LANES), 1) == RANK
    table = jnp.sum(jnp.where(tile, received[:, count:], 0.0), axis=1)
    lane = iota(table.shape, 1)
    valid = lane < sources
    second = pltpu.roll(table, LANES - sources, axis=1)
    third = pltpu.roll(table, LANES - 2 * sources, axis=1)
    reward = jnp.where(valid, table + (second + third), 0.0)
    group = jnp.where(valid, pltpu.roll(table, LANES - 3 * sources, axis=1), -1.0)
    sums = [
        jnp.sum(jnp.where(group == float(i), reward, 0.0), axis=0, keepdims=True)
        for i in range(total // GROUP_MEMBERS)
    ]
    sums = jnp.sum(jnp.concatenate(sums, axis=0), axis=1, keepdims=True) * (1.0 / GROUP_MEMBERS)
    baseline = jnp.zeros_like(reward)
    for i in range(total // GROUP_MEMBERS):
        baseline = jnp.where(group == float(i), sums[i : i + 1, :], baseline)
    centered = jnp.where(valid, reward - baseline, 0.0)
    spread = sum_all(centered * centered) * (1.0 / total)
    shaped = centered / jnp.sqrt(spread + 1e-05)
    mine = jnp.where((iota(table.shape, 0) == place[1]) & (lane == place[0]), shaped, 0.0)
    fitness[...] = sum_all(mine)

    chosen = iota((count, LANES), 1) == iota((count, LANES), 0) // RANK
    weights = jnp.where(chosen[None], jnp.broadcast_to(shaped[:, None, :], (members, count, LANES)), 0.0)
    weighted = received[:, :count] * jnp.sum(weights, axis=2, keepdims=True)
    high = weighted.astype(BF16)
    low = (weighted - high.astype(F32)).astype(BF16)
    half = members // 2
    flat = half * count
    columns = [block[start : start + half].reshape(flat, LANES) for start in (0, half) for block in (high, low)]
    columns = jnp.concatenate(columns, axis=1)
    product = jnp.dot(down[...], columns, preferred_element_type=F32)
    middle = LANES // 2
    first = product[:middle, :LANES] + product[:middle, LANES : 2 * LANES]
    second = product[middle:, 2 * LANES : 3 * LANES] + product[middle:, 3 * LANES :]
    block = ((first + second) * (1.0 / math.sqrt(RANK * total)))[: out.shape[1]]
    out[...] = jnp.broadcast_to(block.astype(BF16)[None], out.shape)


def assemble_kernel(blocks, out_hbm, out, sems):
    sources, share, _ = blocks.shape
    column_parts = out.shape[1] // LANES
    copies = []
    for i in range(sources // column_parts):
        rows = pl.ds(i * share, share)
        for j in range(column_parts):
            out[rows, j * LANES : (j + 1) * LANES] = blocks[i * column_parts + j].astype(F32)
        copies.append(pltpu.make_async_copy(out.at[rows], out_hbm.at[rows], sems.at[i]))
        copies[-1].start()
    for copy in copies:
        copy.wait()


def call(kernel, out_shape, in_specs, *operands, scratch=(), vmem=40, out_spec=VMEM):
    many = isinstance(out_shape, (list, tuple))
    return pl.pallas_call(
        kernel,
        out_shape=out_shape,
        in_specs=in_specs,
        out_specs=[out_spec] * len(out_shape) if many else out_spec,
        scratch_shapes=scratch,
        compiler_params=pltpu.CompilerParams(vmem_limit_bytes=vmem * 1024 * 1024),
    )(*operands)


def exchange(array, axes):
    return lax.all_to_all(array, axes, split_axis=0, concat_axis=0, tiled=True)


def local(
    prompt_states,
    norm_gain,
    kv_weight,
    probe_keys,
    probe_values,
    down_factors,
    up_factors,
    group_ids,
):
    pop = lax.axis_size(XY)
    mp = lax.axis_size(ZC)
    place = jnp.stack([lax.axis_index(XY), lax.axis_index(ZC), group_ids[0]]).astype(jnp.int32)
    states, down, up = prompt_states[0], down_factors[0], up_factors[0]
    tokens, width = states.shape
    columns = up.shape[1]
    rows = width // mp
    share = rows * columns // (pop * LANES)
    heads = 2 * KV_HEADS
    operands = (kv_weight, probe_keys, probe_values, up, down)
    up_probe, parts = call(
        probe_kernel,
        [
            jax.ShapeDtypeStruct((heads, RANK), F32),
            jax.ShapeDtypeStruct((mp, 5 * heads, LANES), BF16),
        ],
        [pl.BlockSpec(memory_space=pltpu.HBM)] * len(operands),
        *operands,
        scratch=[pltpu.VMEM(a.shape, a.dtype) for a in operands] + [pltpu.SemaphoreType.DMA((len(operands),))],
        vmem=60,
    )
    parts = exchange(parts, ZC)
    normed, low = call(
        norm_kernel,
        [jax.ShapeDtypeStruct((tokens, width), BF16), jax.ShapeDtypeStruct((RANK, tokens), F32)],
        [VMEM] * 3,
        states,
        norm_gain[None],
        down,
    )
    half = mp * RANK // 2
    pieces = call(
        reward_kernel,
        jax.ShapeDtypeStruct((pop, half + SUBLANES, LANES), BF16),
        [SMEM] + [VMEM] * 5,
        place,
        normed,
        low,
        parts,
        up_probe,
        up,
    )
    pieces = exchange(pieces, XY)
    ups = call(relay_kernel, jax.ShapeDtypeStruct((mp // 2, pop * RANK + SUBLANES, LANES), BF16), [VMEM], pieces)
    ups = exchange(ups, "z")
    other_ups = lax.ppermute(ups, "core", [(0, 1), (1, 0)])
    downs = call(order_kernel, jax.ShapeDtypeStruct((LANES, mp // 2 * pop * RANK), BF16), [VMEM], pieces)
    fitness, blocks = call(
        update_kernel,
        [jax.ShapeDtypeStruct((1, 1), F32), jax.ShapeDtypeStruct((pop, share, LANES), BF16)],
        [SMEM, VMEM, VMEM, VMEM],
        place,
        ups,
        other_ups,
        downs,
    )
    blocks = exchange(blocks, XY)
    update = call(
        assemble_kernel,
        jax.ShapeDtypeStruct((rows, columns), F32),
        [VMEM],
        blocks,
        scratch=[pltpu.VMEM((rows, columns), F32), pltpu.SemaphoreType.DMA((pop * LANES // columns,))],
        out_spec=pl.BlockSpec(memory_space=pltpu.HBM),
    )
    return (fitness.reshape(1), update)


def solution(mesh):
    grid = Mesh(mesh.devices.reshape(4, 8, 8, 2), ALL)
    in_specs = (
        P(ALL, None, None),
        P(),
        P(ZC, None),
        P(),
        P(),
        P(ALL, None, None),
        P(ALL, None, None),
        P(ALL),
    )
    out_specs = (P(ALL), P(ZC, None))
    return jax.shard_map(local, mesh=grid, in_specs=in_specs, out_specs=out_specs, check_vma=False)
```

```python
import math

import jax
import jax.numpy as jnp
from jax import lax
from jax.experimental import pallas as pl
from jax.experimental.pallas import tpu as pltpu
from jax.sharding import Mesh
from jax.sharding import PartitionSpec as P

KV_HEADS = 4
HEAD = 128
RANK = 4
GROUP_MEMBERS = 16
LANES = 128
SUBLANES = 8
XY = ("y", "x")
ZC = ("z", "core")
ALL = ("x", "y", "z", "core")
VMEM = pl.BlockSpec(memory_space=pltpu.VMEM)
SMEM = pl.BlockSpec(memory_space=pltpu.SMEM)
F32 = jnp.float32
BF16 = jnp.bfloat16
CONTRACT_LANES = (((1,), (1,)), ((), ()))


def bf16_parts(value, count):
    parts = []
    for _ in range(count):
        part = value.astype(BF16).astype(F32)
        parts.append(part)
        value = value - part
    return parts


def iota(shape, axis):
    return lax.broadcasted_iota(jnp.int32, shape, axis)


def sum_all(value):
    return jnp.sum(jnp.sum(value, axis=1, keepdims=True), axis=0, keepdims=True)


def pair_upper(even, odd):
    return jnp.where(iota(even.shape, even.ndim - 2) < RANK, even, pltpu.roll(odd, RANK, axis=odd.ndim - 2))


def pair_lower(even, odd):
    return jnp.where(iota(even.shape, even.ndim - 2) < RANK, pltpu.roll(even, RANK, axis=even.ndim - 2), odd)


def probe_rows(probe_keys, probe_values):
    probes = jnp.concatenate([probe_keys[...], probe_values[...]], axis=0)
    wide = jnp.concatenate([probes] * probes.shape[0], axis=1)
    own = iota(wide.shape, 1) // HEAD == iota(wide.shape, 0)
    return jnp.concatenate(bf16_parts(jnp.where(own, wide, 0.0), 3), axis=0).astype(BF16)


def against_probes(block, probes):
    product = lax.dot_general(probes, block, CONTRACT_LANES, preferred_element_type=F32)
    heads = product.shape[0] // 3
    return product[:heads] + (product[heads : 2 * heads] + product[2 * heads :])


def placed(block, offset):
    shape = (SUBLANES, RANK)
    select = jnp.where(iota(shape, 0) == iota(shape, 1) + offset, 1.0, 0.0).astype(BF16)
    return jnp.dot(select, block, preferred_element_type=F32)


def probe_kernel(weight_hbm, keys_hbm, values_hbm, up_hbm, down_hbm, up_probe, out, *scratch):
    buffers, sems = scratch[:5], scratch[5]
    sources = (weight_hbm, keys_hbm, values_hbm, up_hbm, down_hbm)
    copies = [pltpu.make_async_copy(a, b, sems.at[i]) for i, (a, b) in enumerate(zip(sources, buffers))]
    for copy in copies:
        copy.start()
    weight, probe_keys, probe_values, up, down = buffers
    for copy in copies[1:]:
        copy.wait()
    probes = probe_rows(probe_keys, probe_values)
    up_probe[...] = against_probes(up[...], probes)
    devices = out.shape[0]
    rows = weight.shape[0]
    first = placed(down[...], 0)
    second = jnp.concatenate([placed(down[...], RANK), jnp.zeros((SUBLANES, LANES), F32)], axis=1)
    copies[0].wait()
    product = jnp.concatenate(bf16_parts(against_probes(weight[...], probes), 2), axis=0)
    spare = jnp.zeros((product.shape[0], 2 * LANES - rows), F32)
    product = jnp.concatenate([product[:, :LANES], jnp.concatenate([product[:, LANES:], spare], axis=1)], axis=0)
    for i in range(devices):
        start = (i % (devices // 2) * 2 + i // (devices // 2)) * rows
        block = first[:, start : start + LANES] + second[:, start + LANES : start + 2 * LANES]
        out[i] = jnp.concatenate([product, block], axis=0).astype(BF16)


def norm_kernel(states, gain, down, normed, low):
    values = states[...].astype(F32)
    scale = lax.rsqrt(jnp.mean(values * values, axis=-1, keepdims=True) + 1e-06)
    normed[...] = (values * scale * gain[...]).astype(BF16)
    low[...] = lax.dot_general(down[...], normed[...], CONTRACT_LANES, preferred_element_type=F32)


def reward_kernel(place, normed, low, received, up_probe, up, out):
    received = received[...].astype(F32)
    members = received.shape[0]
    heads = 2 * KV_HEADS
    rest = normed.shape[1] // members - LANES
    probe = []
    for i in range(members):
        source = received[i % 2 * (members // 2) + i // 2]
        probe += [source[: 2 * heads], source[2 * heads : 4 * heads, :rest]]
    probe = jnp.concatenate(probe, axis=1).astype(BF16)
    score = lax.dot_general(probe, normed[...], CONTRACT_LANES, preferred_element_type=F32)
    score = score[:heads] + score[heads:]
    extra = up_probe[:, 0:1] * low[0:1, :]
    for i in range(1, RANK):
        extra = extra + up_probe[:, i : i + 1] * low[i : i + 1, :]
    score = (score + 0.0025 * extra) * (1.0 / math.sqrt(HEAD))
    terms = jnp.tanh(score[:KV_HEADS]) * score[KV_HEADS:]
    reward = sum_all(terms) * (1.0 / terms.shape[1])

    targets = out.shape[0]
    tile = (SUBLANES, LANES)
    lane = iota(tile, 1)
    row = jnp.where(lane == place[0] + 3 * targets, place[2].astype(F32), 0.0)
    for i, part in enumerate(bf16_parts(reward, 3)):
        row = row + jnp.where(lane == place[0] + i * targets, part, 0.0)
    row = jnp.where(iota(tile, 0) == RANK, row, 0.0)

    down = received[:, 4 * heads :].reshape(2, members // 2, SUBLANES, LANES)
    first = pair_upper(down[0], down[1]).reshape(members * RANK, LANES)
    second = pair_lower(down[0], down[1]).reshape(members * RANK, LANES)
    down = jnp.concatenate([first, second[:, :rest]], axis=1)
    half = members * RANK // 2
    column_parts = up.shape[1] // LANES
    row_parts = targets // column_parts
    share = down.shape[1] // row_parts
    spare = jnp.zeros((half, LANES // 2 - share), F32)
    ups = placed(up[...], 0)
    for i in range(row_parts):
        mine = down[:, i * share : (i + 1) * share]
        mine = jnp.concatenate([mine[:half], spare, mine[half:], spare], axis=1)
        for j in range(column_parts):
            last = ups[:, j * LANES : (j + 1) * LANES] + row
            out[j * row_parts + i] = jnp.concatenate([mine, last], axis=0).astype(BF16)


def relay_kernel(received, out):
    last = received[...].astype(F32)
    last = last[:, last.shape[1] - SUBLANES :]
    row = jnp.sum(last, axis=0)
    last = last.reshape(last.shape[0] // 2, 2, SUBLANES, LANES)
    ups = pair_upper(last[:, 0], last[:, 1])
    block = jnp.concatenate([ups.reshape(-1, LANES), row], axis=0).astype(BF16)
    out[...] = jnp.broadcast_to(block[None], out.shape)


def order_kernel(received, out):
    sources, rows, _ = received.shape
    tiles = rows // SUBLANES - 1
    down = received[...].astype(F32)[:, : tiles * SUBLANES]
    down = down.reshape(sources // 2, 2, tiles, SUBLANES, LANES)
    for core, pair in enumerate((pair_upper, pair_lower)):
        ordered = pair(down[:, 0], down[:, 1])
        ordered = [ordered[:, i].reshape(-1, LANES) for i in range(tiles)]
        out[core] = jnp.transpose(jnp.concatenate(ordered, axis=0)).astype(BF16)


def update_kernel(place, own, other, down, fitness, out):
    chips, rows, _ = own.shape
    count = rows - SUBLANES
    sources = count // RANK
    total = 2 * chips * sources
    tile = iota((chips, SUBLANES, LANES), 1) == RANK
    table = [jnp.sum(jnp.where(tile, ref[...].astype(F32)[:, count:], 0.0), axis=1) for ref in (own, other)]
    table = jnp.concatenate(table, axis=0)
    lane = iota(table.shape, 1)
    valid = lane < sources
    second = pltpu.roll(table, LANES - sources, axis=1)
    third = pltpu.roll(table, LANES - 2 * sources, axis=1)
    reward = jnp.where(valid, table + (second + third), 0.0)
    group = jnp.where(valid, pltpu.roll(table, LANES - 3 * sources, axis=1), -1.0)
    sums = [
        jnp.sum(jnp.where(group == float(i), reward, 0.0), axis=0, keepdims=True)
        for i in range(total // GROUP_MEMBERS)
    ]
    sums = jnp.sum(jnp.concatenate(sums, axis=0), axis=1, keepdims=True) * (1.0 / GROUP_MEMBERS)
    baseline = jnp.zeros_like(reward)
    for i in range(total // GROUP_MEMBERS):
        baseline = jnp.where(group == float(i), sums[i : i + 1, :], baseline)
    centered = jnp.where(valid, reward - baseline, 0.0)
    spread = sum_all(centered * centered) * (1.0 / total)
    shaped = centered / jnp.sqrt(spread + 1e-05)
    mine = (iota(table.shape, 0) == place[1] // 2) & (lane == place[0])
    fitness[...] = sum_all(jnp.where(mine, shaped, 0.0))

    each = jnp.where(iota((LANES, count), 0) == iota((LANES, count), 1) // RANK, 1.0, 0.0).astype(BF16)
    weights = jnp.concatenate(bf16_parts(shaped, 3), axis=0).astype(BF16)
    weights = jnp.dot(weights, each, preferred_element_type=F32)
    weights = weights[: 2 * chips] + (weights[2 * chips : 4 * chips] + weights[4 * chips :])
    half = chips // 2
    middle = LANES // 2
    flat = half * count
    core = place[1] % 2
    product = jnp.zeros((2 * LANES, 2 * LANES), F32)
    for i, (which, ref) in enumerate(((core, own), (1 - core, other))):
        scale = []
        for j in range(half):
            first = i * chips + j
            rows_of = [jnp.broadcast_to(weights[k : k + 1], (middle, count)) for k in (first, first + half)]
            scale.append(jnp.concatenate(rows_of, axis=0))
        weighted = down[which].astype(F32) * jnp.concatenate(scale, axis=1)
        high = weighted.astype(BF16)
        low = (weighted - high.astype(F32)).astype(BF16)
        ups = ref[...].astype(F32)[:, :count]
        ups = [ups[start : start + half].reshape(flat, LANES) for start in (0, half)]
        ups = jnp.concatenate(ups, axis=1).astype(BF16)
        parts = jnp.concatenate([high, low], axis=0)
        product = product + jnp.dot(parts, ups, preferred_element_type=F32)
    first = product[:middle, :LANES] + product[LANES : LANES + middle, :LANES]
    second = product[middle:LANES, LANES:] + product[LANES + middle :, LANES:]
    block = ((first + second) * (1.0 / math.sqrt(RANK * total)))[: out.shape[1]]
    out[...] = jnp.broadcast_to(block.astype(BF16)[None], out.shape)


def assemble_kernel(blocks, out_hbm, out, sems):
    sources, share, _ = blocks.shape
    column_parts = out.shape[1] // LANES
    row_parts = sources // column_parts
    copies = []
    for i in range(row_parts):
        rows = pl.ds(i * share, share)
        for j in range(column_parts):
            out[rows, j * LANES : (j + 1) * LANES] = blocks[j * row_parts + i].astype(F32)
        copies.append(pltpu.make_async_copy(out.at[rows], out_hbm.at[rows], sems.at[i]))
        copies[-1].start()
    for copy in copies:
        copy.wait()


def call(kernel, out_shape, in_specs, *operands, scratch=(), vmem=40, out_spec=VMEM):
    many = isinstance(out_shape, (list, tuple))
    return pl.pallas_call(
        kernel,
        out_shape=out_shape,
        in_specs=in_specs,
        out_specs=[out_spec] * len(out_shape) if many else out_spec,
        scratch_shapes=scratch,
        compiler_params=pltpu.CompilerParams(vmem_limit_bytes=vmem * 1024 * 1024),
    )(*operands)


def exchange(array, axes):
    return lax.all_to_all(array, axes, split_axis=0, concat_axis=0, tiled=True)


def local(
    prompt_states,
    norm_gain,
    kv_weight,
    probe_keys,
    probe_values,
    down_factors,
    up_factors,
    group_ids,
):
    pop = lax.axis_size(XY)
    mp = lax.axis_size(ZC)
    place = jnp.stack([lax.axis_index(XY), lax.axis_index(ZC), group_ids[0]]).astype(jnp.int32)
    states, down, up = prompt_states[0], down_factors[0], up_factors[0]
    tokens, width = states.shape
    columns = up.shape[1]
    rows = width // mp
    share = rows * columns // (pop * LANES)
    heads = 2 * KV_HEADS
    operands = (kv_weight, probe_keys, probe_values, up, down)
    up_probe, parts = call(
        probe_kernel,
        [
            jax.ShapeDtypeStruct((heads, RANK), F32),
            jax.ShapeDtypeStruct((mp, 5 * heads, LANES), BF16),
        ],
        [pl.BlockSpec(memory_space=pltpu.HBM)] * len(operands),
        *operands,
        scratch=[pltpu.VMEM(a.shape, a.dtype) for a in operands] + [pltpu.SemaphoreType.DMA((len(operands),))],
        vmem=60,
    )
    parts = exchange(parts, ("core", "z"))
    normed, low = call(
        norm_kernel,
        [jax.ShapeDtypeStruct((tokens, width), BF16), jax.ShapeDtypeStruct((RANK, tokens), F32)],
        [VMEM] * 3,
        states,
        norm_gain[None],
        down,
    )
    half = mp * RANK // 2
    pieces = call(
        reward_kernel,
        jax.ShapeDtypeStruct((pop, half + SUBLANES, LANES), BF16),
        [SMEM] + [VMEM] * 5,
        place,
        normed,
        low,
        parts,
        up_probe,
        up,
    )
    pieces = exchange(pieces, XY)
    ups = call(relay_kernel, jax.ShapeDtypeStruct((mp // 2, pop * RANK + SUBLANES, LANES), BF16), [VMEM], pieces)
    ups = exchange(ups, "z")
    other_ups = lax.ppermute(ups, "core", [(0, 1), (1, 0)])
    downs = call(order_kernel, jax.ShapeDtypeStruct((2, LANES, mp // 4 * pop * RANK), BF16), [VMEM], pieces)
    fitness, blocks = call(
        update_kernel,
        [jax.ShapeDtypeStruct((1, 1), F32), jax.ShapeDtypeStruct((pop, share, LANES), BF16)],
        [SMEM, VMEM, VMEM, VMEM],
        place,
        ups,
        other_ups,
        downs,
    )
    blocks = exchange(blocks, XY)
    update = call(
        assemble_kernel,
        jax.ShapeDtypeStruct((rows, columns), F32),
        [VMEM],
        blocks,
        scratch=[pltpu.VMEM((rows, columns), F32), pltpu.SemaphoreType.DMA((pop * LANES // columns,))],
        out_spec=pl.BlockSpec(memory_space=pltpu.HBM),
    )
    return (fitness.reshape(1), update)


def solution(mesh):
    grid = Mesh(mesh.devices.reshape(4, 8, 8, 2), ALL)
    in_specs = (
        P(ALL, None, None),
        P(),
        P(ZC, None),
        P(),
        P(),
        P(ALL, None, None),
        P(ALL, None, None),
        P(ALL),
    )
    out_specs = (P(ALL), P(ZC, None))
    return jax.shard_map(local, mesh=grid, in_specs=in_specs, out_specs=out_specs, check_vma=False)
```

```python
import math

import jax
import jax.numpy as jnp
from jax import lax
from jax.experimental import pallas as pl
from jax.experimental.pallas import tpu as pltpu
from jax.sharding import Mesh
from jax.sharding import PartitionSpec as P

KV_HEADS = 4
HEAD = 128
RANK = 4
GROUP_MEMBERS = 16
LANES = 128
SUBLANES = 8
XY = ("y", "x")
ZC = ("z", "core")
ALL = ("x", "y", "z", "core")
VMEM = pl.BlockSpec(memory_space=pltpu.VMEM)
SMEM = pl.BlockSpec(memory_space=pltpu.SMEM)
F32 = jnp.float32
BF16 = jnp.bfloat16
CONTRACT_LANES = (((1,), (1,)), ((), ()))


def bf16_parts(value, count):
    parts = []
    for _ in range(count):
        part = value.astype(BF16).astype(F32)
        parts.append(part)
        value = value - part
    return parts


def iota(shape, axis):
    return lax.broadcasted_iota(jnp.int32, shape, axis)


def sum_all(value):
    return jnp.sum(jnp.sum(value, axis=1, keepdims=True), axis=0, keepdims=True)


def pair_upper(even, odd):
    return jnp.where(iota(even.shape, even.ndim - 2) < RANK, even, pltpu.roll(odd, RANK, axis=odd.ndim - 2))


def pair_lower(even, odd):
    return jnp.where(iota(even.shape, even.ndim - 2) < RANK, pltpu.roll(even, RANK, axis=even.ndim - 2), odd)


def probe_rows(probe_keys, probe_values):
    probes = jnp.concatenate([probe_keys[...], probe_values[...]], axis=0)
    wide = jnp.concatenate([probes] * probes.shape[0], axis=1)
    own = iota(wide.shape, 1) // HEAD == iota(wide.shape, 0)
    return jnp.concatenate(bf16_parts(jnp.where(own, wide, 0.0), 3), axis=0).astype(BF16)


def against_probes(block, probes):
    product = lax.dot_general(probes, block, CONTRACT_LANES, preferred_element_type=F32)
    heads = product.shape[0] // 3
    return product[:heads] + (product[heads : 2 * heads] + product[2 * heads :])


def placed(block, offset):
    shape = (SUBLANES, RANK)
    select = jnp.where(iota(shape, 0) == iota(shape, 1) + offset, 1.0, 0.0).astype(BF16)
    return jnp.dot(select, block, preferred_element_type=F32)


def probe_kernel(weight_hbm, keys_hbm, values_hbm, up_hbm, down_hbm, up_probe, out, *scratch):
    buffers, sems = scratch[:5], scratch[5]
    sources = (weight_hbm, keys_hbm, values_hbm, up_hbm, down_hbm)
    copies = [pltpu.make_async_copy(a, b, sems.at[i]) for i, (a, b) in enumerate(zip(sources, buffers))]
    for copy in copies:
        copy.start()
    weight, probe_keys, probe_values, up, down = buffers
    for copy in copies[1:]:
        copy.wait()
    probes = probe_rows(probe_keys, probe_values)
    up_probe[...] = against_probes(up[...], probes)
    devices = out.shape[0]
    rows = weight.shape[0]
    first = placed(down[...], 0)
    second = jnp.concatenate([placed(down[...], RANK), jnp.zeros((SUBLANES, LANES), F32)], axis=1)
    copies[0].wait()
    product = jnp.concatenate(bf16_parts(against_probes(weight[...], probes), 2), axis=0)
    spare = jnp.zeros((product.shape[0], 2 * LANES - rows), F32)
    product = jnp.concatenate([product[:, :LANES], jnp.concatenate([product[:, LANES:], spare], axis=1)], axis=0)
    for i in range(devices):
        start = (i % (devices // 2) * 2 + i // (devices // 2)) * rows
        block = first[:, start : start + LANES] + second[:, start + LANES : start + 2 * LANES]
        out[i] = jnp.concatenate([product, block], axis=0).astype(BF16)


def norm_kernel(states, gain, down, normed, low):
    values = states[...].astype(F32)
    scale = lax.rsqrt(jnp.mean(values * values, axis=-1, keepdims=True) + 1e-06)
    normed[...] = (values * scale * gain[...]).astype(BF16)
    low[...] = lax.dot_general(down[...], normed[...], CONTRACT_LANES, preferred_element_type=F32)


def reward_kernel(place, normed, low, received, up_probe, up, out):
    received = received[...].astype(F32)
    members = received.shape[0]
    heads = 2 * KV_HEADS
    rest = normed.shape[1] // members - LANES
    probe = []
    for i in range(members):
        source = received[i % 2 * (members // 2) + i // 2]
        probe += [source[: 2 * heads], source[2 * heads : 4 * heads, :rest]]
    probe = jnp.concatenate(probe, axis=1).astype(BF16)
    score = lax.dot_general(probe, normed[...], CONTRACT_LANES, preferred_element_type=F32)
    score = score[:heads] + score[heads:]
    extra = up_probe[:, 0:1] * low[0:1, :]
    for i in range(1, RANK):
        extra = extra + up_probe[:, i : i + 1] * low[i : i + 1, :]
    score = (score + 0.0025 * extra) * (1.0 / math.sqrt(HEAD))
    terms = jnp.tanh(score[:KV_HEADS]) * score[KV_HEADS:]
    reward = sum_all(terms) * (1.0 / terms.shape[1])

    targets = out.shape[0]
    tile = (SUBLANES, LANES)
    lane = iota(tile, 1)
    row = jnp.where(lane == place[0] + 3 * targets, place[2].astype(F32), 0.0)
    for i, part in enumerate(bf16_parts(reward, 3)):
        row = row + jnp.where(lane == place[0] + i * targets, part, 0.0)
    row = jnp.where(iota(tile, 0) == RANK, row, 0.0)

    down = received[:, 4 * heads :].reshape(2, members // 2, SUBLANES, LANES)
    first = pair_upper(down[0], down[1]).reshape(members * RANK, LANES)
    second = pair_lower(down[0], down[1]).reshape(members * RANK, LANES)
    down = jnp.concatenate([first, second[:, :rest]], axis=1)
    half = members * RANK // 2
    column_parts = up.shape[1] // LANES
    row_parts = targets // column_parts
    share = down.shape[1] // row_parts
    spare = jnp.zeros((half, LANES // 2 - share), F32)
    ups = placed(up[...], 0)
    for i in range(row_parts):
        mine = down[:, i * share : (i + 1) * share]
        mine = jnp.concatenate([mine[:half], spare, mine[half:], spare], axis=1)
        for j in range(column_parts):
            last = ups[:, j * LANES : (j + 1) * LANES] + row
            out[j * row_parts + i] = jnp.concatenate([mine, last], axis=0).astype(BF16)


def relay_kernel(received, out):
    last = received[...].astype(F32)
    last = last[:, last.shape[1] - SUBLANES :]
    row = jnp.sum(last, axis=0)
    last = last.reshape(last.shape[0] // 2, 2, SUBLANES, LANES)
    ups = pair_upper(last[:, 0], last[:, 1])
    block = jnp.concatenate([ups.reshape(-1, LANES), row], axis=0).astype(BF16)
    out[...] = jnp.broadcast_to(block[None], out.shape)


def order_kernel(received, out):
    sources, rows, _ = received.shape
    tiles = rows // SUBLANES - 1
    down = received[...].astype(F32)[:, : tiles * SUBLANES]
    down = down.reshape(sources // 2, 2, tiles, SUBLANES, LANES)
    for core, pair in enumerate((pair_upper, pair_lower)):
        ordered = pair(down[:, 0], down[:, 1])
        ordered = [ordered[:, i].reshape(-1, LANES) for i in range(tiles)]
        out[core] = jnp.transpose(jnp.concatenate(ordered, axis=0)).astype(BF16)


def update_kernel(place, own, other, down, fitness, out):
    chips, rows, _ = own.shape
    count = rows - SUBLANES
    sources = count // RANK
    total = 2 * chips * sources
    tile = iota((chips, SUBLANES, LANES), 1) == RANK
    table = [jnp.sum(jnp.where(tile, ref[...].astype(F32)[:, count:], 0.0), axis=1) for ref in (own, other)]
    table = jnp.concatenate(table, axis=0)
    lane = iota(table.shape, 1)
    valid = lane < sources
    second = pltpu.roll(table, LANES - sources, axis=1)
    third = pltpu.roll(table, LANES - 2 * sources, axis=1)
    reward = jnp.where(valid, table + (second + third), 0.0)
    group = jnp.where(valid, pltpu.roll(table, LANES - 3 * sources, axis=1), -1.0)
    sums = [
        jnp.sum(jnp.where(group == float(i), reward, 0.0), axis=0, keepdims=True)
        for i in range(total // GROUP_MEMBERS)
    ]
    sums = jnp.sum(jnp.transpose(jnp.concatenate(sums, axis=0)), axis=0, keepdims=True) * (1.0 / GROUP_MEMBERS)
    spare = jnp.zeros((1, LANES - sums.shape[1]), F32)
    means = jnp.broadcast_to(jnp.concatenate([sums, spare], axis=1), table.shape)
    chosen = jnp.where(valid, group, 0.0).astype(jnp.int32)
    baseline = jnp.take_along_axis(means, chosen, axis=1, mode="promise_in_bounds")
    centered = jnp.where(valid, reward - baseline, 0.0)
    spread = sum_all(centered * centered) * (1.0 / total)
    shaped = centered / jnp.sqrt(spread + 1e-05)
    mine = (iota(table.shape, 0) == place[1] // 2) & (lane == place[0])
    fitness[...] = sum_all(jnp.where(mine, shaped, 0.0))

    each = jnp.where(iota((LANES, count), 0) == iota((LANES, count), 1) // RANK, 1.0, 0.0).astype(BF16)
    weights = jnp.concatenate(bf16_parts(shaped, 3), axis=0).astype(BF16)
    weights = jnp.dot(weights, each, preferred_element_type=F32)
    weights = weights[: 2 * chips] + (weights[2 * chips : 4 * chips] + weights[4 * chips :])
    half = chips // 2
    middle = LANES // 2
    flat = half * count
    core = place[1] % 2
    product = jnp.zeros((2 * LANES, 2 * LANES), F32)
    for i, (which, ref) in enumerate(((core, own), (1 - core, other))):
        scale = []
        for j in range(half):
            first = i * chips + j
            rows_of = [jnp.broadcast_to(weights[k : k + 1], (middle, count)) for k in (first, first + half)]
            scale.append(jnp.concatenate(rows_of, axis=0))
        weighted = down[which].astype(F32) * jnp.concatenate(scale, axis=1)
        high = weighted.astype(BF16)
        low = (weighted - high.astype(F32)).astype(BF16)
        ups = ref[...].astype(F32)[:, :count]
        ups = [ups[start : start + half].reshape(flat, LANES) for start in (0, half)]
        ups = jnp.concatenate(ups, axis=1).astype(BF16)
        parts = jnp.concatenate([high, low], axis=0)
        product = product + jnp.dot(parts, ups, preferred_element_type=F32)
    first = product[:middle, :LANES] + product[LANES : LANES + middle, :LANES]
    second = product[middle:LANES, LANES:] + product[LANES + middle :, LANES:]
    block = ((first + second) * (1.0 / math.sqrt(RANK * total)))[: out.shape[1]]
    out[...] = jnp.broadcast_to(block.astype(BF16)[None], out.shape)


def assemble_kernel(blocks, out_hbm, out, sems):
    sources, share, _ = blocks.shape
    column_parts = out.shape[1] // LANES
    row_parts = sources // column_parts
    copies = []
    for i in range(row_parts):
        rows = pl.ds(i * share, share)
        for j in range(column_parts):
            out[rows, j * LANES : (j + 1) * LANES] = blocks[j * row_parts + i].astype(F32)
        copies.append(pltpu.make_async_copy(out.at[rows], out_hbm.at[rows], sems.at[i]))
        copies[-1].start()
    for copy in copies:
        copy.wait()


def call(kernel, out_shape, in_specs, *operands, scratch=(), vmem=40, out_spec=VMEM):
    many = isinstance(out_shape, (list, tuple))
    return pl.pallas_call(
        kernel,
        out_shape=out_shape,
        in_specs=in_specs,
        out_specs=[out_spec] * len(out_shape) if many else out_spec,
        scratch_shapes=scratch,
        compiler_params=pltpu.CompilerParams(vmem_limit_bytes=vmem * 1024 * 1024),
    )(*operands)


def exchange(array, axes):
    return lax.all_to_all(array, axes, split_axis=0, concat_axis=0, tiled=True)


def local(
    prompt_states,
    norm_gain,
    kv_weight,
    probe_keys,
    probe_values,
    down_factors,
    up_factors,
    group_ids,
):
    pop = lax.axis_size(XY)
    mp = lax.axis_size(ZC)
    place = jnp.stack([lax.axis_index(XY), lax.axis_index(ZC), group_ids[0]]).astype(jnp.int32)
    states, down, up = prompt_states[0], down_factors[0], up_factors[0]
    tokens, width = states.shape
    columns = up.shape[1]
    rows = width // mp
    share = rows * columns // (pop * LANES)
    heads = 2 * KV_HEADS
    operands = (kv_weight, probe_keys, probe_values, up, down)
    up_probe, parts = call(
        probe_kernel,
        [
            jax.ShapeDtypeStruct((heads, RANK), F32),
            jax.ShapeDtypeStruct((mp, 5 * heads, LANES), BF16),
        ],
        [pl.BlockSpec(memory_space=pltpu.HBM)] * len(operands),
        *operands,
        scratch=[pltpu.VMEM(a.shape, a.dtype) for a in operands] + [pltpu.SemaphoreType.DMA((len(operands),))],
        vmem=60,
    )
    parts = exchange(parts, ("core", "z"))
    normed, low = call(
        norm_kernel,
        [jax.ShapeDtypeStruct((tokens, width), BF16), jax.ShapeDtypeStruct((RANK, tokens), F32)],
        [VMEM] * 3,
        states,
        norm_gain[None],
        down,
    )
    half = mp * RANK // 2
    pieces = call(
        reward_kernel,
        jax.ShapeDtypeStruct((pop, half + SUBLANES, LANES), BF16),
        [SMEM] + [VMEM] * 5,
        place,
        normed,
        low,
        parts,
        up_probe,
        up,
    )
    pieces = exchange(pieces, XY)
    ups = call(relay_kernel, jax.ShapeDtypeStruct((mp // 2, pop * RANK + SUBLANES, LANES), BF16), [VMEM], pieces)
    ups = exchange(ups, "z")
    other_ups = lax.ppermute(ups, "core", [(0, 1), (1, 0)])
    downs = call(order_kernel, jax.ShapeDtypeStruct((2, LANES, mp // 4 * pop * RANK), BF16), [VMEM], pieces)
    fitness, blocks = call(
        update_kernel,
        [jax.ShapeDtypeStruct((1, 1), F32), jax.ShapeDtypeStruct((pop, share, LANES), BF16)],
        [SMEM, VMEM, VMEM, VMEM],
        place,
        ups,
        other_ups,
        downs,
    )
    blocks = exchange(blocks, XY)
    update = call(
        assemble_kernel,
        jax.ShapeDtypeStruct((rows, columns), F32),
        [VMEM],
        blocks,
        scratch=[pltpu.VMEM((rows, columns), F32), pltpu.SemaphoreType.DMA((pop * LANES // columns,))],
        out_spec=pl.BlockSpec(memory_space=pltpu.HBM),
    )
    return (fitness.reshape(1), update)


def solution(mesh):
    grid = Mesh(mesh.devices.reshape(4, 8, 8, 2), ALL)
    in_specs = (
        P(ALL, None, None),
        P(),
        P(ZC, None),
        P(),
        P(),
        P(ALL, None, None),
        P(ALL, None, None),
        P(ALL),
    )
    out_specs = (P(ALL), P(ZC, None))
    return jax.shard_map(local, mesh=grid, in_specs=in_specs, out_specs=out_specs, check_vma=False)
```
